32 devices in a mesh: groups: 2 (over y), adapter: 8 (over z, x), tensor: 2 (over core).
Axes of the slice: x: 2, y: 2, z: 4, core: 2. Of those that a mesh axis runs over, the one named last changes fastest.
Arguments:
- tokens: bfloat16 [4096, 8192], P(('groups', 'adapter'), 'tensor'), parts along dimension 0, may hold values from -6 to 6
- kv_weight: bfloat16 [8192, 1024], P(None, 'tensor'), may hold values from -0.0625 to 0.0625
- down_a: bfloat16 [32, 8192, 64], P(('groups', 'adapter')), parts along dimension 0, may hold values from -0.0625 to 0.0625
- up_weight: bfloat16 [32, 64, 1024], P(('groups', 'adapter')), parts along dimension 0, may hold values from -0.75 to 0.75
- adapter_ids: int32 [112], P(('groups', 'adapter')), parts along dimension 0, may hold values from 0 to 15, as said below
- lengths: int32 [112], P(('groups', 'adapter')), parts along dimension 0, may hold values from 1 to 73, as said below
Outputs:
- values_out: bfloat16 [4096, 1024], P(('groups', 'adapter'), 'tensor'), parts along dimension 0
The draws below stay inside these ranges and needn't reach their ends.
There are 2 independent parts, one for each index of `groups`. The reference program is written for one: setup_inputs(seed, part) draws one part's arguments, and reference() takes and returns one part's arrays. A program takes and returns all parts, laid end to end along the dimension named above; an argument that names none is the same for every part. Nothing has to cross between parts.
Inputs may be any that keep to these rules, and one draw needn't show every extreme that they name: The 7 requests of one index of adapter (consecutive entries) have prompt lengths summing to 256; exactly one of them has length 73, every other one at most 31, and one of those exactly 31. `adapter_ids`: the owner of adapter a is a // 2. The 7 requests of one index of adapter name adapters of 7 different owners. In each part the request of length 73 names the same owner on every index of adapter.
All inputs are finite; a program needn't handle non-finite values.
Results may differ from the reference program's by a relative error of at most 0.0055.
Values may be sent and summed in bfloat16 or wider, within the bound.
No kernel may reach another device: no remote copies, remote signals or barrier semaphores. Data moves between devices by JAX's collectives and lax.ppermute only.
A program may use at most 128 MiB of HBM per device.

```python
import jax
import jax.numpy as jnp
from jax import lax

D = 8192
KV = 1024
R = 64
TOK_DEV = 256
ADAPT_DEV = 2
REQ_DEV = 7
MOST = 73
COLD = 31
PROMPT_TOKENS = 2048
REQS = 56
ADAPTERS = 16


def request_layout(key):
    owner_total = REQS // REQ_DEV
    key_list = jax.random.split(key, owner_total + 1)
    hot_owner = jax.random.randint(key_list[0], (), 0, owner_total)
    spare = (REQ_DEV - 2) * (COLD - 1)
    extra_total = TOK_DEV - MOST - (REQ_DEV - 1) - (COLD - 1)

    def one_device(dev_key):
        parts_key = jax.random.split(dev_key, 4)
        ranking = jax.random.permutation(parts_key[0], spare)
        chosen = (ranking < extra_total).astype(jnp.int32)
        extras = chosen.reshape(REQ_DEV - 2, COLD - 1).sum(axis=1)
        lengths_all = jnp.concatenate([jnp.full((1,), MOST, jnp.int32), jnp.full((1,), COLD, jnp.int32), 1 + extras])
        others = jax.random.permutation(parts_key[1], owner_total - 1)[:REQ_DEV - 1]
        others = others + (others >= hot_owner).astype(jnp.int32)
        owners_all = jnp.concatenate([jnp.full((1,), hot_owner, jnp.int32), others.astype(jnp.int32)])
        offset_by = jax.random.randint(parts_key[2], (), 0, REQ_DEV)
        lengths_all = jnp.roll(lengths_all, offset_by)
        owners_all = jnp.roll(owners_all, offset_by)
        local_pick = jax.random.randint(parts_key[3], (REQ_DEV,), 0, ADAPT_DEV)
        return (lengths_all.astype(jnp.int32), (owners_all * ADAPT_DEV + local_pick).astype(jnp.int32))
    lengths_all, ids_all = jax.vmap(one_device)(key_list[1:])
    return (lengths_all.reshape(-1), ids_all.reshape(-1))


def draw_lengths(key, part):
    return request_layout(key)[0]


def draw_adapter_ids(key, part):
    return request_layout(key)[1]


def block_levels(rng, extent, cuts, least, largest):
    def one(dim, shards_of):
        heights = jax.random.uniform(jax.random.fold_in(jax.random.fold_in(rng, 6), dim), (shards_of,), jnp.float32, least / len(cuts), largest / len(cuts))
        return jnp.repeat(jnp.exp(heights), extent[dim] // shards_of).reshape((-1,) + (1,) * (len(extent) - dim - 1))

    factor_of = one(*cuts[0])
    for cut in cuts[1:]:
        factor_of = factor_of * one(*cut)
    return factor_of


def gaussian(rng, extent, deviation, reach, pieces=(), kind=jnp.bfloat16):
    result = jax.random.normal(rng, extent, jnp.float32) * deviation
    if len(pieces) > 0:
        result = block_levels(rng, extent, pieces, -0.22, 0.18) * result
    return jnp.clip(result, min=-reach, max=reach).astype(kind)


def setup_inputs(seed: int = 0, part: int = 0) -> dict:
    streams_of = jax.random.split(jax.random.key(seed), 7)
    part_splits = jax.random.split(jax.random.fold_in(streams_of[6], part), 7)
    return {
        "tokens": gaussian(part_splits[0], (PROMPT_TOKENS, D), 1.0, 6.0, ((0, 8), (1, 2))),
        "kv_weight": gaussian(streams_of[1], (D, KV), D ** -0.5, 0.0625, ((1, 2),)),
        "down_a": gaussian(part_splits[2], (ADAPTERS, D, R), D ** -0.5, 0.0625, ((0, 8),)),
        "up_weight": gaussian(part_splits[3], (ADAPTERS, R, KV), R ** -0.5, 0.75, ((0, 8),)),
        "adapter_ids": draw_adapter_ids(jax.random.fold_in(jax.random.fold_in(streams_of[6], part), 71), part),
        "lengths": draw_lengths(jax.random.fold_in(jax.random.fold_in(streams_of[6], part), 71), part),
    }


adapter_scale = 2.0


def reference(tokens, kv_weight, down_a, up_weight, adapter_ids, lengths):
    base_output = jnp.dot(tokens, kv_weight, preferred_element_type=jnp.float32)
    ends = jnp.cumsum(lengths).astype(jnp.int32)
    starts = (ends - lengths).astype(jnp.int32)
    padded = jnp.concatenate([tokens, jnp.zeros((MOST, D), jnp.bfloat16)], axis=0)
    slot_pos = jnp.arange(MOST, dtype=jnp.int32)

    def request_step(delta_total, request):
        start_row = starts[request].astype(jnp.int32)
        length_now = lengths[request]
        adapter_now = adapter_ids[request]
        block_rows = lax.dynamic_slice_in_dim(padded, start_row, MOST, 0)
        low_rank = jnp.dot(block_rows, down_a[adapter_now], preferred_element_type=jnp.float32)
        rounded_length = low_rank.astype(jnp.bfloat16)
        delta_rows = jnp.dot(rounded_length, up_weight[adapter_now], preferred_element_type=jnp.float32)
        delta_rows = delta_rows.astype(jnp.bfloat16).astype(jnp.float32)
        previous = lax.dynamic_slice_in_dim(delta_total, start_row, MOST, 0)
        updated = jnp.where((slot_pos < length_now)[:, None], delta_rows, previous)
        return lax.dynamic_update_slice_in_dim(delta_total, updated, start_row, 0), None

    delta_init = jnp.zeros((PROMPT_TOKENS + MOST, KV), jnp.float32)
    delta_total, _ = lax.scan(request_step, delta_init, jnp.arange(REQS, dtype=jnp.int32))
    return (base_output + adapter_scale * delta_total[:PROMPT_TOKENS]).astype(jnp.bfloat16)
```

```python
import jax
import jax.numpy as jnp
from jax import lax
from jax.sharding import PartitionSpec as P

adapter_scale = 2.0
bf16 = jnp.bfloat16
f32 = jnp.float32
swap_bit = 2
chunk_count = 4


def dot(left, right, contract):
    return lax.dot_general(left, right, ((contract[:1], contract[1:]), ((), ())), preferred_element_type=f32)


def shards(tokens, kv_weight, down_a, up_weight, adapter_ids, lengths):
    owners = lax.axis_size("adapter")
    me = lax.axis_index("adapter")
    core = lax.axis_index("tensor")
    adapt_dev, width, rank = down_a.shape
    both = adapt_dev * rank
    rows, half = tokens.shape
    heads = kv_weight.shape[1]
    req_dev = lengths.shape[0]
    most = 2 * rows // req_dev
    cold = -(-(rows - most) // (req_dev - 1))
    slots = min(rows, most + (owners // 2 - 1) * cold)
    slots = -(-slots // 16) * 16

    def flip(x, bit):
        return lax.ppermute(x, "adapter", [(j, j ^ bit) for j in range(owners)])

    def other_core(x):
        return lax.ppermute(x, "tensor", [(0, 1), (1, 0)])

    down_t = jnp.transpose(down_a, (0, 2, 1)).reshape(both, width)
    step = half // chunk_count
    pieces = {0: [lax.dynamic_slice(down_t, (0, core * half + c * step), (both, step)) for c in range(chunk_count)]}
    up_mine = lax.dynamic_slice(up_weight.reshape(both, -1), (0, core * heads), (both, heads))
    pieces[0][0] = jnp.concatenate([pieces[0][0], up_mine], axis=1)

    q = jnp.arange(req_dev, dtype=jnp.int32)
    upto = q[None, :] <= q[:, None]
    ends = jnp.sum(jnp.where(upto, lengths[None, :], 0), axis=1)
    starts = ends - lengths
    away_q = (((adapter_ids // adapt_dev) ^ me) & swap_bit) != 0
    away_len = jnp.where(away_q, lengths, 0)
    offset = jnp.sum(jnp.where(upto, away_len[None, :], 0), axis=1) - away_len
    r = jnp.arange(rows, dtype=jnp.int32)
    inside = (starts[None, :] <= r[:, None]) & (r[:, None] < ends[None, :])
    row_adapter = jnp.sum(jnp.where(inside, adapter_ids[None, :], 0), axis=1)
    place = jnp.sum(jnp.where(inside & away_q[None, :], (offset - starts + 1)[None, :] + r[:, None], 0), axis=1) - 1
    s = jnp.arange(slots, dtype=jnp.int32)
    hit = s[:, None] == place[None, :]
    pick = hit.astype(bf16)
    sent = dot(pick, tokens, (1, 0)).astype(bf16)
    sent_adapter = jnp.sum(jnp.where(hit, row_adapter[None, :], 0), axis=1)

    got_adapter = flip(sent_adapter, swap_bit)
    got = flip(sent, swap_bit)
    tokens_other = other_core(tokens)

    bits = [1 << b for b in range(owners.bit_length() - 1)]
    for bit in [b for b in bits if b > swap_bit] + [b for b in bits if b < swap_bit]:
        for m in list(pieces):
            pieces[m | bit] = [flip(c, bit) for c in pieces[m]]

    base = dot(tokens, lax.dynamic_slice(kv_weight, (core * half, 0), (half, heads)), (1, 0))
    base = base + dot(tokens_other, lax.dynamic_slice(kv_weight, ((1 - core) * half, 0), (half, heads)), (1, 0))

    def low_rank_part(x, which):
        total = jnp.zeros((x.shape[0], both), f32)
        for m, chunks in pieces.items():
            term = sum(dot(x[:, c * step : (c + 1) * step], chunks[c][:, :step], (1, 1)) for c in range(chunk_count))
            total = total + jnp.where((which // adapt_dev == (me ^ m))[:, None], term, 0.0)
        lane = jnp.arange(both, dtype=jnp.int32) // rank
        return jnp.where((which % adapt_dev)[:, None] == lane[None, :], total, 0.0)

    up_all = jnp.concatenate([chunks[0][:, step:] for chunks in pieces.values()], axis=0)

    def delta_of(low, which):
        spread = jnp.concatenate(
            [jnp.where((which // adapt_dev == (me ^ m))[:, None], low, jnp.zeros((), bf16)) for m in pieces], axis=1
        )
        return dot(spread, up_all, (1, 0)).astype(bf16)

    part_got = low_rank_part(got, got_adapter)
    part_own = low_rank_part(tokens, row_adapter)
    low_got = (part_got + other_core(part_got)).astype(bf16)
    low_own = (part_own + other_core(part_own)).astype(bf16)
    delta_got = delta_of(low_got, got_adapter)
    back = flip(delta_got, swap_bit)
    delta_own = delta_of(low_own, row_adapter)
    delta = delta_own.astype(f32) + dot(pick, back, (0, 0))
    return (base + adapter_scale * delta).astype(bf16)


def solution(mesh):
    placed = (
        P(("groups", "adapter"), "tensor"),
        P(None, "tensor"),
        P(("groups", "adapter"), None, None),
        P(("groups", "adapter"), None, None),
        P(("groups", "adapter")),
        P(("groups", "adapter")),
    )
    return jax.shard_map(
        shards,
        mesh=mesh,
        in_specs=placed,
        out_specs=P(("groups", "adapter"), "tensor"),
        check_vma=False,
    )
```

```python
import functools
import math

import jax
import jax.numpy as jnp
from jax import lax
from jax.experimental import pallas as pl
from jax.experimental.pallas import tpu as pltpu
from jax.sharding import PartitionSpec as P

adapter_scale = 2.0
bf16 = jnp.bfloat16
f32 = jnp.float32
i32 = jnp.int32
swap_bit = 2
chunk_parts = (10, 6)
vmem_limit = 48 * 1024 * 1024
smem = pl.BlockSpec(memory_space=pltpu.SMEM)


def dot(left, right, contract=(1, 0)):
    return lax.dot_general(left, right, ((contract[:1], contract[1:]), ((), ())), preferred_element_type=f32)


def requests(len_ref, id_ref, me, adapt_dev):
    first, slot = 0, 0
    for q in range(len_ref.shape[0]):
        length, adapter = len_ref[q], id_ref[q]
        away = jnp.where((((adapter // adapt_dev) ^ me) & swap_bit) != 0, length, 0)
        yield first, length, adapter, slot, away
        first, slot = first + length, slot + away


def row_places(reqs, shape, dim):
    r = lax.broadcasted_iota(i32, shape, dim)
    place = jnp.full(shape, -1, i32)
    for first, _, _, slot, away in reqs:
        place = jnp.where((r >= first) & (r < first + away), r - first + slot, place)
    return place


def pack_kernel(adapt_dev, me_ref, len_ref, id_ref, tok_ref, out_ref):
    slots, step = out_ref.shape
    rows = tok_ref.shape[0]
    reqs = list(requests(len_ref, id_ref, me_ref[0], adapt_dev))
    hit = lax.broadcasted_iota(i32, (slots, rows), 0) == row_places(reqs, (1, rows), 1)
    packed = dot(hit.astype(f32).astype(bf16), tok_ref[...])
    col = lax.broadcasted_iota(i32, (1, step), 1) + pl.program_id(0) * step
    adapter_of = jnp.zeros((1, step), i32)
    for _, _, adapter, slot, away in reqs:
        adapter_of = jnp.where((col >= slot) & (col < slot + away), adapter, adapter_of)
    last = lax.broadcasted_iota(i32, (slots, step), 0) == slots - 1
    out_ref[...] = jnp.where(last, adapter_of.astype(f32), packed).astype(bf16)


def cut_kernel(spans, at_ref, down_ref, up_ref, *out_refs):
    *part_refs, mine_ref = out_refs
    heads = up_ref.shape[1]
    for c, (start, size) in enumerate(spans):
        values = down_ref[:, start : start + size]
        part_refs[c][:, :size] = values
        behind = heads if c else 0
        mine_ref[:, start + behind : start + behind + size] = values
    size = spans[0][1]
    part_refs[0][:, size:] = up_ref[...]
    mine_ref[:, size : size + heads] = up_ref[...]


def own_adapters(reqs, rows, both):
    r = lax.broadcasted_iota(i32, (rows, both), 0)
    adapter_of = jnp.zeros((rows, both), i32)
    for first, length, adapter, _, _ in reqs:
        adapter_of = jnp.where((r >= first) & (r < first + length), adapter, adapter_of)
    return adapter_of


def got_adapters(head, both):
    slots, wide = head.shape
    slot = lax.broadcasted_iota(i32, (slots, wide), 0)
    named = jnp.sum(jnp.where(slot == slots - 1, head.astype(f32), 0.0), axis=0, keepdims=True)
    col = lax.broadcasted_iota(i32, (slots, wide), 1)
    across = jnp.sum(jnp.where(slot == col, named, 0.0), axis=1, keepdims=True)
    return jnp.broadcast_to(across, (slots, both)).astype(i32)


def low_kernel(adapt_dev, rank, plan, block, sets, count_x, with_sums, joined, *refs):
    me_ref, len_ref, id_ref, *refs = refs
    me = me_ref[0]
    head_ref = refs.pop(0) if "got" in sets else None
    x_refs = {}
    for name in sets:
        x_refs[name], refs = refs[:count_x], refs[count_x:]
    out_refs = [refs.pop()] * len(sets) if joined else [refs.pop(-len(sets) + k) for k in range(len(sets))]
    sum_refs = [refs.pop(-len(sets) + k) for k in range(len(sets))] if with_sums else None
    at = 0
    for k, name in enumerate(sets):
        count, both = x_refs[name][0].shape[0], out_refs[k].shape[1]
        if name == "own":
            which = own_adapters(list(requests(len_ref, id_ref, me, adapt_dev)), count, both)
        else:
            which = got_adapters(head_ref[...], both)
        total = sum_refs[k][...] if with_sums else jnp.zeros((count, both), f32)
        for m, ref_no, blocks in plan:
            term = None
            for start, col, size in blocks:
                for j in range(0, size, block):
                    more = dot(x_refs[name][(start + j) // block][...], refs[ref_no][:, col + j : col + j + block], (1, 1))
                    term = more if term is None else term + more
            total = total + jnp.where(which // adapt_dev == (me ^ m), term, 0.0)
        if joined:
            lane = lax.broadcasted_iota(i32, (count, both), 1)
            out_refs[k][at : at + count, :] = jnp.where(which % adapt_dev == lane // rank, total, 0.0)
            at += count
        else:
            out_refs[k][...] = total


def up_kernel(adapt_dev, marks, me_ref, len_ref, id_ref, head_ref, part_ref, other_ref, *refs):
    up_refs, (own_ref, got_ref) = refs[:-2], refs[-2:]
    rows, slots = own_ref.shape[0], got_ref.shape[0]
    both = part_ref.shape[1]
    me = me_ref[0]
    own_which = own_adapters(list(requests(len_ref, id_ref, me, adapt_dev)), rows, both)
    got_which = got_adapters(head_ref[...], both)
    for which, out_ref, at, count in ((got_which, got_ref, rows, slots), (own_which, own_ref, 0, rows)):
        low = (part_ref[at : at + count, :] + other_ref[at : at + count, :]).astype(bf16).astype(f32)
        total = None
        for m, up_ref in zip(marks, up_refs, strict=True):
            term = dot(jnp.where(which // adapt_dev == (me ^ m), low, 0.0).astype(bf16), up_ref[...])
            total = term if total is None else total + term
        out_ref[...] = total.astype(bf16)


def last_kernel(adapt_dev, me_ref, len_ref, id_ref, base_ref, own_ref, back_ref, out_ref):
    rows, slots = own_ref.shape[0], back_ref.shape[0]
    reqs = list(requests(len_ref, id_ref, me_ref[0], adapt_dev))
    hit = row_places(reqs, (rows, slots), 0) == lax.broadcasted_iota(i32, (rows, slots), 1)
    delta = own_ref[...].astype(f32) + dot(hit.astype(f32).astype(bf16), back_ref[...])
    out_ref[...] = (base_ref[...] + adapter_scale * delta).astype(bf16)


def whole(x):
    return pl.BlockSpec(x.shape, lambda *_: (0,) * x.ndim)


def columns(x, start, size):
    return pl.BlockSpec((x.shape[0], size), lambda *_: (0, start // size))


def after(x, *others):
    return lax.optimization_barrier((x, *others))[0]


def shards(tokens, kv_weight, down_a, up_weight, adapter_ids, lengths):
    owners = lax.axis_size("adapter")
    core = lax.axis_index("tensor")
    adapt_dev, width, rank = down_a.shape
    both = adapt_dev * rank
    rows, half = tokens.shape
    heads = kv_weight.shape[1]
    req_dev = lengths.shape[0]
    most = 2 * rows // req_dev
    cold = -(-(rows - most) // (req_dev - 1))
    slots = min(rows, most + (owners // 2 - 1) * cold) + 1
    slots = -(-slots // 8) * 8
    head_wide = -(-slots // 128) * 128
    me = lax.axis_index("adapter").astype(i32).reshape(1)
    scalars = (me, lengths, adapter_ids)
    params = pltpu.CompilerParams(vmem_limit_bytes=vmem_limit)

    def flip(x, bit):
        return lax.ppermute(x, "adapter", [(j, j ^ bit) for j in range(owners)])

    def other_core(x):
        return lax.ppermute(x, "tensor", [(0, 1), (1, 0)])

    sizes = [half * p // 16 for p in chunk_parts]
    spans = [(sum(sizes[:c]), size) for c, size in enumerate(sizes)]
    widths = [size + (heads if c == 0 else 0) for c, size in enumerate(sizes)] + [half + heads]
    *parts, mine = pl.pallas_call(
        functools.partial(cut_kernel, spans),
        grid_spec=pltpu.PrefetchScalarGridSpec(
            num_scalar_prefetch=1,
            grid=(1,),
            in_specs=[
                pl.BlockSpec((both, half), lambda _, at: (0, at[0])),
                pl.BlockSpec((both, heads), lambda _, at: (0, at[0])),
            ],
            out_specs=[pl.BlockSpec((both, w), lambda _, at: (0, 0)) for w in widths],
        ),
        out_shape=[jax.ShapeDtypeStruct((both, w), bf16) for w in widths],
        compiler_params=params,
        name="cut",
    )(
        core.astype(i32).reshape(1),
        jnp.transpose(down_a, (0, 2, 1)).reshape(both, width),
        up_weight.reshape(both, -1),
    )

    tokens_other = other_core(after(tokens, mine))

    sent = pl.pallas_call(
        functools.partial(pack_kernel, adapt_dev),
        grid=(4,),
        out_shape=jax.ShapeDtypeStruct((slots, half), bf16),
        in_specs=[smem] * 3 + [pl.BlockSpec((rows, half // 4), lambda g: (0, g))],
        out_specs=pl.BlockSpec((slots, half // 4), lambda g: (0, g)),
        compiler_params=params,
        name="pack",
    )(*scalars, after(tokens, tokens_other))
    got = flip(sent, swap_bit)

    bits = [1 << b for b in range(owners.bit_length() - 1)]
    single = [(mine, [(c, a + (heads if c else 0)) for c, (a, _) in enumerate(spans)])]
    split = [(part, [(c, 0)]) for c, part in enumerate(parts)]
    pieces = {0: single}
    for bit in [b for b in bits if b > swap_bit]:
        for m in list(pieces):
            pieces[m | bit] = [(flip(x, bit), places) for x, places in (split if m == 0 else pieces[m])]
    near = flip(after(mine, sent), 1)

    base_own = dot(tokens, lax.dynamic_slice(kv_weight, (core * half, 0), (half, heads)))
    base = base_own + dot(tokens_other, lax.dynamic_slice(kv_weight, ((1 - core) * half, 0), (half, heads)))

    row_arrays = {"own": tokens, "got": got}

    def add_low(sets, sums, group, joined=False):
        used = sorted({c for _, _, places in group for c, _ in places})
        lowest, above = spans[used[0]][0], sum(spans[used[-1]])
        block = math.gcd(half, *(edge for c in used for edge in spans[c]), lowest)
        at = range(lowest, above, block)
        plan = [
            (m, k, [(spans[c][0] - lowest, col, spans[c][1]) for c, col in places])
            for k, (m, _, places) in enumerate(group)
        ]
        xs = [row_arrays[name] for name in sets]
        tail = [x for _, x, _ in group] + list(sums or [])
        head = [got] if "got" in sets else []
        counts = [rows + slots] if joined else [x.shape[0] for x in xs]
        flops = sum(2 * x.shape[0] * both * size for x in xs for _, _, blocks in plan for _, _, size in blocks)
        return pl.pallas_call(
            functools.partial(low_kernel, adapt_dev, rank, plan, block, sets, len(at), bool(sums), joined),
            grid=(1,),
            out_shape=[jax.ShapeDtypeStruct((n, both), f32) for n in counts],
            in_specs=[smem] * 3
            + [columns(got, 0, head_wide) for _ in head]
            + [columns(x, a, block) for x in xs for a in at]
            + [whole(x) for x in tail],
            out_specs=[pl.BlockSpec((n, both), lambda *_: (0, 0)) for n in counts],
            compiler_params=params,
            cost_estimate=pl.CostEstimate(flops=4 * flops, bytes_accessed=flops // 64, transcendentals=0),
            name="low",
        )(*scalars, *head, *[x for x in xs for _ in at], *tail)

    pieces[1] = [(near, single[0][1])]
    far = [(m, x, places) for m, piece in pieces.items() if m & ~1 and not m & 1 for x, places in piece]
    far.sort(key=lambda item: item[2][0][0])
    batch = max(3, owners // 8)
    groups = [[(0, mine, single[0][1]), (1, near, single[0][1]), far[0]]]
    own = add_low(("own",), None, groups[0])[0]
    rest = []
    for k, (m, x, places) in enumerate(far):
        last = places[0][0] == len(spans) - 1
        across = flip(after(x, own, base) if last else after(x, base_own), 1)
        pieces.setdefault(m | 1, []).append((across, places))
        rest.extend([(m, x, places), (m | 1, across, places)][0 if k else 1 :])
    groups = groups + [rest[a : min(a + batch, len(rest) - 1)] for a in range(0, len(rest) - 1, batch)]
    sums = [own, add_low(("got",), None, groups[0])[0]]
    for group in groups[1:]:
        sums = add_low(("own", "got"), sums, group)
    sums = add_low(("own", "got"), sums, rest[-1:], True)[0]

    other = other_core(sums)
    ups = [piece[0][0] for piece in pieces.values()]
    delta_own, delta_got = pl.pallas_call(
        functools.partial(up_kernel, adapt_dev, list(pieces)),
        grid=(1,),
        out_shape=[jax.ShapeDtypeStruct((count, heads), bf16) for count in (rows, slots)],
        in_specs=[smem] * 3
        + [columns(got, 0, head_wide), whole(sums), whole(other)]
        + [columns(x, sizes[0], heads) for x in ups],
        out_specs=[pl.BlockSpec((count, heads), lambda *_: (0, 0)) for count in (rows, slots)],
        compiler_params=params,
        name="up",
    )(*scalars, got, sums, other, *ups)
    back = flip(delta_got, swap_bit)
    return pl.pallas_call(
        functools.partial(last_kernel, adapt_dev),
        grid=(1,),
        out_shape=jax.ShapeDtypeStruct((rows, heads), bf16),
        in_specs=[smem] * 3 + [whole(base), whole(delta_own), whole(back)],
        out_specs=pl.BlockSpec((rows, heads), lambda *_: (0, 0)),
        compiler_params=params,
        name="last",
    )(*scalars, base, delta_own, back)


def solution(mesh):
    placed = (
        P(("groups", "adapter"), "tensor"),
        P(None, "tensor"),
        P(("groups", "adapter"), None, None),
        P(("groups", "adapter"), None, None),
        P(("groups", "adapter")),
        P(("groups", "adapter")),
    )
    return jax.shard_map(
        shards,
        mesh=mesh,
        in_specs=placed,
        out_specs=P(("groups", "adapter"), "tensor"),
        check_vma=False,
    )
```

```python
import functools
import math

import jax
import jax.numpy as jnp
from jax import lax
from jax.experimental import pallas as pl
from jax.experimental.pallas import tpu as pltpu
from jax.sharding import PartitionSpec as P

adapter_scale = 2.0
bf16 = jnp.bfloat16
f32 = jnp.float32
i32 = jnp.int32
swap_bit = 2
chunk_parts = (7, 5, 4)
up_chunk = 0
halves = 2
vmem_limit = 48 * 1024 * 1024
smem = pl.BlockSpec(memory_space=pltpu.SMEM)


def dot(left, right, contract=(1, 0)):
    return lax.dot_general(left, right, ((contract[:1], contract[1:]), ((), ())), preferred_element_type=f32)


def requests(len_ref, id_ref, me, adapt_dev):
    first, slot = 0, 0
    for q in range(len_ref.shape[0]):
        length, adapter = len_ref[q], id_ref[q]
        away = jnp.where((((adapter // adapt_dev) ^ me) & swap_bit) != 0, length, 0)
        yield first, length, adapter, slot, away
        first, slot = first + length, slot + away


def row_places(reqs, shape, dim):
    r = lax.broadcasted_iota(i32, shape, dim)
    place = jnp.full(shape, -1, i32)
    for first, _, _, slot, away in reqs:
        place = jnp.where((r >= first) & (r < first + away), r - first + slot, place)
    return place


def start_kernel(adapt_dev, spans, with_up, len_ref, id_ref, tok_ref, down_ref, up_ref, *refs):
    sent_refs, (*part_refs, mine_ref, sems) = refs[:halves], refs[halves:]
    half = sum(size for _, size in spans)
    heads = mine_ref.shape[1] - half
    core = lax.axis_index("tensor")

    def features(start, size):
        return down_ref.at[:, pl.ds(pl.multiple_of(core * half + start, 128), size)]

    up = up_ref.at[:, pl.ds(pl.multiple_of(core * heads, 128), heads)]
    moves = []
    for c, (start, size) in enumerate(spans):
        ahead = heads if c == with_up else 0
        moves.append((features(start, size), part_refs[c].at[:, pl.ds(ahead, size)]))
    moves.append((up, part_refs[with_up].at[:, pl.ds(0, heads)]))
    moves.append((up, mine_ref.at[:, pl.ds(0, heads)]))
    moves.append((features(0, half), mine_ref.at[:, pl.ds(heads, half)]))
    copies = [pltpu.make_async_copy(source, target, sems.at[k]) for k, (source, target) in enumerate(moves)]

    @pl.when(pl.program_id(0) == 0)
    def _():
        for copy in copies:
            copy.start()

    slots, step = sent_refs[0].shape
    rows = tok_ref.shape[0]
    reqs = list(requests(len_ref, id_ref, lax.axis_index("adapter"), adapt_dev))
    hit = lax.broadcasted_iota(i32, (slots, rows), 0) == row_places(reqs, (1, rows), 1)
    packed = dot(hit.astype(f32).astype(bf16), tok_ref[...])
    col = lax.broadcasted_iota(i32, (1, step), 1) + pl.program_id(0) * step
    adapter_of = jnp.zeros((1, step), i32)
    for _, _, adapter, slot, away in reqs:
        adapter_of = jnp.where((col >= slot) & (col < slot + away), adapter, adapter_of)
    last = lax.broadcasted_iota(i32, (slots, step), 0) == slots - 1
    packed = jnp.where(last, adapter_of.astype(f32), packed).astype(bf16)
    for part, sent_ref in enumerate(sent_refs):

        @pl.when(pl.program_id(0) == part)
        def _():
            sent_ref[...] = packed

    @pl.when(pl.program_id(0) == halves - 1)
    def _():
        for copy in copies:
            copy.wait()


def own_adapters(reqs, rows, both):
    r = lax.broadcasted_iota(i32, (rows, both), 0)
    adapter_of = jnp.zeros((rows, both), i32)
    for first, length, adapter, _, _ in reqs:
        adapter_of = jnp.where((r >= first) & (r < first + length), adapter, adapter_of)
    return adapter_of


def got_adapters(head, both):
    slots, wide = head.shape
    slot = lax.broadcasted_iota(i32, (slots, wide), 0)
    named = jnp.sum(jnp.where(slot == slots - 1, head.astype(f32), 0.0), axis=0, keepdims=True)
    col = lax.broadcasted_iota(i32, (slots, wide), 1)
    across = jnp.sum(jnp.where(slot == col, named, 0.0), axis=1, keepdims=True)
    return jnp.broadcast_to(across, (slots, both)).astype(i32)


def which_adapters(adapt_dev, me_ref, len_ref, id_ref, head_refs, shape):
    if head_refs:
        return got_adapters(head_refs[0][...], shape[1])
    return own_adapters(list(requests(len_ref, id_ref, me_ref[0], adapt_dev)), *shape)


def low_kernel(adapt_dev, rank, plan, block, heads_in, x_count, first, final, me_ref, len_ref, id_ref, *refs):
    head_refs, refs = refs[:heads_in], refs[heads_in:]
    x_refs, refs, out_ref = refs[:x_count], refs[x_count:-1], refs[-1]
    which = which_adapters(adapt_dev, me_ref, len_ref, id_ref, head_refs, out_ref.shape)
    me = me_ref[0]
    total = jnp.zeros(out_ref.shape, f32) if first else refs[-1][...]
    for m, ref_no, blocks in plan:
        term = None
        for start, col, size in blocks:
            for j in range(0, size, block):
                down = refs[ref_no][:, col + j : col + j + block]
                more = dot(x_refs[(start + j) // block][...], down, (1, 1))
                term = more if term is None else term + more
        total = total + jnp.where(which // adapt_dev == (me ^ m), term, 0.0)
    if final:
        lane = lax.broadcasted_iota(i32, out_ref.shape, 1)
        total = jnp.where(which % adapt_dev == lane // rank, total, 0.0)
    out_ref[...] = total


def up_kernel(adapt_dev, marks, heads_in, me_ref, len_ref, id_ref, *refs):
    head_refs, refs = refs[:heads_in], refs[heads_in:]
    part_ref, other_ref, *refs, out_ref = refs
    which = which_adapters(adapt_dev, me_ref, len_ref, id_ref, head_refs, part_ref.shape)
    low = (part_ref[...] + other_ref[...]).astype(bf16).astype(f32)
    total = None
    for m, up_ref in zip(marks, refs):
        term = dot(jnp.where(which // adapt_dev == (me_ref[0] ^ m), low, 0.0).astype(bf16), up_ref[...])
        total = term if total is None else total + term
    delta = total.astype(bf16)
    if heads_in:
        out_ref[...] = delta
    else:
        out_ref[...] = refs[-1][...] + adapter_scale * delta.astype(f32)


def last_kernel(adapt_dev, me_ref, len_ref, id_ref, sum_ref, back_ref, out_ref):
    rows, slots = sum_ref.shape[0], back_ref.shape[0]
    reqs = list(requests(len_ref, id_ref, me_ref[0], adapt_dev))
    hit = row_places(reqs, (rows, slots), 0) == lax.broadcasted_iota(i32, (rows, slots), 1)
    delta = dot(hit.astype(f32).astype(bf16), back_ref[...])
    out_ref[...] = (sum_ref[...] + adapter_scale * delta).astype(bf16)


def whole(x):
    return pl.BlockSpec(x.shape, lambda *_: (0,) * x.ndim)


def columns(x, start, size):
    return pl.BlockSpec((x.shape[0], size), lambda *_: (0, start // size))


def after(x, *others):
    return lax.optimization_barrier((x, *others))[0]


def shards(tokens, kv_weight, down_a, up_weight, adapter_ids, lengths):
    owners = lax.axis_size("adapter")
    core = lax.axis_index("tensor")
    adapt_dev, width, rank = down_a.shape
    both = adapt_dev * rank
    rows, half = tokens.shape
    heads = kv_weight.shape[1]
    req_dev = lengths.shape[0]
    most = 2 * rows // req_dev
    cold = -(-(rows - most) // (req_dev - 1))
    slots = min(rows, most + (owners // 2 - 1) * cold) + 1
    slots = -(-slots // 8) * 8
    head_wide = -(-slots // 128) * 128
    me = lax.axis_index("adapter").astype(i32).reshape(1)
    scalars = (me, lengths, adapter_ids)
    params = pltpu.CompilerParams(vmem_limit_bytes=vmem_limit)

    def flip(x, bit):
        return lax.ppermute(x, "adapter", [(j, j ^ bit) for j in range(owners)])

    def other_core(x):
        return lax.ppermute(x, "tensor", [(0, 1), (1, 0)])

    sizes = [half * p // 16 for p in chunk_parts]
    spans = [(sum(sizes[:c]), size) for c, size in enumerate(sizes)]
    widths = [size + (heads if c == up_chunk else 0) for c, size in enumerate(sizes)] + [half + heads]
    sent_shapes = [jax.ShapeDtypeStruct((slots, half // halves), bf16)] * halves
    *outs, mine = pl.pallas_call(
        functools.partial(start_kernel, adapt_dev, spans, up_chunk),
        grid=(halves,),
        out_shape=sent_shapes + [jax.ShapeDtypeStruct((both, w), bf16) for w in widths],
        in_specs=[smem] * 2
        + [pl.BlockSpec((rows, half // halves), lambda g: (0, g))]
        + [pl.BlockSpec(memory_space=pl.ANY)] * 2,
        out_specs=[pl.BlockSpec((slots, half // halves), lambda *_: (0, 0))] * halves
        + [pl.BlockSpec((both, w), lambda *_: (0, 0)) for w in widths],
        scratch_shapes=[pltpu.SemaphoreType.DMA((len(spans) + 3,))],
        compiler_params=params,
        name="start",
    )(lengths, adapter_ids, tokens, jnp.transpose(down_a, (0, 2, 1)).reshape(both, width), up_weight.reshape(both, -1))
    sent, parts = outs[:halves], outs[halves:]
    tokens_other = other_core(after(tokens, sent[0]))
    got = [flip(after(x, tokens_other), swap_bit) for x in sent]

    bits = [1 << b for b in range(owners.bit_length() - 1)]
    whole_places = [(c, heads + a) for c, (a, _) in enumerate(spans)]
    split = [(part, [(c, heads if c == up_chunk else 0)]) for c, part in enumerate(parts)]
    pieces = {0: [(mine, whole_places)]}
    for bit in [b for b in bits if b > swap_bit]:
        for m in list(pieces):
            came = []
            for c, (x, places) in enumerate(split if m == 0 else pieces[m]):
                came.append((flip(after(x, came[0][0]) if c == 2 else x, bit), places))
            pieces[m | bit] = came
    near = flip(mine, 1)

    base_own = dot(tokens, lax.dynamic_slice(kv_weight, (core * half, 0), (half, heads)))
    base = base_own + dot(tokens_other, lax.dynamic_slice(kv_weight, ((1 - core) * half, 0), (half, heads)))

    def add_low(arrays, heads_in, sums, group, final=False):
        used = sorted({c for _, _, places in group for c, _ in places})
        lowest, above = spans[used[0]][0], sum(spans[used[-1]])
        block = math.gcd(half // halves, *(edge for c in used for edge in spans[c]), lowest)
        at = range(lowest, above, block)
        plan = [
            (m, k, [(spans[c][0] - lowest, col, spans[c][1]) for c, col in places])
            for k, (m, _, places) in enumerate(group)
        ]
        xs = [arrays[a * len(arrays) // half] for a in at]
        x_specs = [columns(x, a % x.shape[1], block) for x, a in zip(xs, at, strict=True)]
        tail = [x for _, x, _ in group] + ([] if sums is None else [sums])
        n = arrays[0].shape[0]
        flops = sum(2 * n * both * size for _, _, blocks in plan for _, _, size in blocks)
        return pl.pallas_call(
            functools.partial(
                low_kernel, adapt_dev, rank, plan, block, len(heads_in), len(xs), sums is None, final
            ),
            grid=(1,),
            out_shape=jax.ShapeDtypeStruct((n, both), f32),
            in_specs=[smem] * 3 + [columns(x, 0, head_wide) for x in heads_in] + x_specs + [whole(x) for x in tail],
            out_specs=pl.BlockSpec((n, both), lambda *_: (0, 0)),
            compiler_params=params,
            cost_estimate=pl.CostEstimate(flops=4 * flops, bytes_accessed=flops // 64, transcendentals=0),
            name="low",
        )(*scalars, *heads_in, *xs, *tail)

    pieces[1] = [(near, whole_places)]
    far = [(m, x, places) for m, piece in pieces.items() if m & ~1 and not m & 1 for x, places in piece]
    far.sort(key=lambda item: item[2][0][0])
    items = [(0, mine, whole_places), (1, near, whole_places), far[0]]
    own = add_low([tokens], [], None, items)
    done = len(items)
    for k, (m, x, places) in enumerate(far):
        last = places[0][0] == len(spans) - 1
        if False:
            own, done = add_low([tokens], [], own, items[3:5]), 5
        across = flip(after(x, own, base) if last else after(x, own if k else base_own), 1)
        pieces.setdefault(m | 1, []).append((across, places))
        items.extend([(m, x, places), (m | 1, across, places)][0 if k else 1 :])

    def low_rank(arrays, heads_in, sums, todo, batch, final):
        rest = len(todo) - final
        for a in range(0, rest, batch):
            sums = add_low(arrays, heads_in, sums, todo[a : min(a + batch, rest)])
        part = add_low(arrays, heads_in, sums, todo[rest:], True)
        return part, other_core(part)

    ups = [next(x for x, places in piece if (up_chunk, heads) == places[-1] or len(places) > 1) for piece in pieces.values()]

    def up(heads_in, lows, extra, kind):
        n = lows[0].shape[0]
        return pl.pallas_call(
            functools.partial(up_kernel, adapt_dev, list(pieces), len(heads_in)),
            grid=(1,),
            out_shape=jax.ShapeDtypeStruct((n, heads), kind),
            in_specs=[smem] * 3
            + [columns(x, 0, head_wide) for x in heads_in]
            + [whole(x) for x in lows]
            + [columns(x, 0, heads) for x in ups]
            + [whole(x) for x in extra],
            out_specs=pl.BlockSpec((n, heads), lambda *_: (0, 0)),
            compiler_params=params,
            name="up",
        )(*scalars, *heads_in, *lows, *ups, *extra)

    low_got = low_rank(got, got[:1], None, items, max(6, owners // 8), 2)
    delta_got = up(got[:1], low_got, [], bf16)
    back = flip(delta_got, swap_bit)
    low_own = low_rank([tokens], [], after(own, delta_got), items[done:], max(5, owners // 8), 5)
    total = up([], low_own, [base], f32)
    return pl.pallas_call(
        functools.partial(last_kernel, adapt_dev),
        grid=(1,),
        out_shape=jax.ShapeDtypeStruct((rows, heads), bf16),
        in_specs=[smem] * 3 + [whole(total), whole(back)],
        out_specs=pl.BlockSpec((rows, heads), lambda *_: (0, 0)),
        compiler_params=params,
        name="last",
    )(*scalars, total, back)


def solution(mesh):
    placed = (
        P(("groups", "adapter"), "tensor"),
        P(None, "tensor"),
        P(("groups", "adapter"), None, None),
        P(("groups", "adapter"), None, None),
        P(("groups", "adapter")),
        P(("groups", "adapter")),
    )
    return jax.shard_map(
        shards,
        mesh=mesh,
        in_specs=placed,
        out_specs=P(("groups", "adapter"), "tensor"),
        check_vma=False,
    )
```

```python
import functools
import math

import jax
import jax.numpy as jnp
from jax import lax
from jax.experimental import pallas as pl
from jax.experimental.pallas import tpu as pltpu
from jax.sharding import PartitionSpec as P

adapter_scale = 2.0
bf16 = jnp.bfloat16
f32 = jnp.float32
i32 = jnp.int32
swap_bit = 2
chunk_parts = (7, 5, 4)
up_chunk = 0
halves = 2
vmem_limit = 48 * 1024 * 1024
smem = pl.BlockSpec(memory_space=pltpu.SMEM)


def dot(left, right, contract=(1, 0)):
    return lax.dot_general(left, right, ((contract[:1], contract[1:]), ((), ())), preferred_element_type=f32)


def requests(len_ref, id_ref, me, adapt_dev):
    first, slot = 0, 0
    for q in range(len_ref.shape[0]):
        length, adapter = len_ref[q], id_ref[q]
        away = jnp.where((((adapter // adapt_dev) ^ me) & swap_bit) != 0, length, 0)
        yield first, length, adapter, slot, away
        first, slot = first + length, slot + away


def row_places(reqs, shape, dim):
    r = lax.broadcasted_iota(i32, shape, dim)
    place = jnp.full(shape, -1, i32)
    for first, _, _, slot, away in reqs:
        place = jnp.where((r >= first) & (r < first + away), r - first + slot, place)
    return place


def start_kernel(adapt_dev, spans, with_up, len_ref, id_ref, tok_ref, down_ref, up_ref, *refs):
    sent_refs, (*part_refs, mine_ref, sems) = refs[:halves], refs[halves:]
    half = sum(size for _, size in spans)
    heads = mine_ref.shape[1] - half
    core = lax.axis_index("tensor")

    def features(start, size):
        return down_ref.at[:, pl.ds(pl.multiple_of(core * half + start, 128), size)]

    up = up_ref.at[:, pl.ds(pl.multiple_of(core * heads, 128), heads)]
    moves = []
    for c, (start, size) in enumerate(spans):
        ahead = heads if c == with_up else 0
        moves.append((features(start, size), part_refs[c].at[:, pl.ds(ahead, size)]))
    moves.append((up, part_refs[with_up].at[:, pl.ds(0, heads)]))
    moves.append((up, mine_ref.at[:, pl.ds(0, heads)]))
    moves.append((features(0, half), mine_ref.at[:, pl.ds(heads, half)]))
    copies = [pltpu.make_async_copy(source, target, sems.at[k]) for k, (source, target) in enumerate(moves)]

    @pl.when(pl.program_id(0) == 0)
    def _():
        for copy in copies:
            copy.start()

    slots, step = sent_refs[0].shape
    rows = tok_ref.shape[0]
    reqs = list(requests(len_ref, id_ref, lax.axis_index("adapter"), adapt_dev))
    hit = lax.broadcasted_iota(i32, (slots, rows), 0) == row_places(reqs, (1, rows), 1)
    packed = dot(hit.astype(f32).astype(bf16), tok_ref[...])
    col = lax.broadcasted_iota(i32, (1, step), 1) + pl.program_id(0) * step
    adapter_of = jnp.zeros((1, step), i32)
    for _, _, adapter, slot, away in reqs:
        adapter_of = jnp.where((col >= slot) & (col < slot + away), adapter, adapter_of)
    last = lax.broadcasted_iota(i32, (slots, step), 0) == slots - 1
    packed = jnp.where(last, adapter_of.astype(f32), packed).astype(bf16)
    for part, sent_ref in enumerate(sent_refs):

        @pl.when(pl.program_id(0) == part)
        def _():
            sent_ref[...] = packed

    @pl.when(pl.program_id(0) == halves - 1)
    def _():
        for copy in copies:
            copy.wait()


def own_adapters(reqs, rows, both):
    r = lax.broadcasted_iota(i32, (rows, both), 0)
    adapter_of = jnp.zeros((rows, both), i32)
    for first, length, adapter, _, _ in reqs:
        adapter_of = jnp.where((r >= first) & (r < first + length), adapter, adapter_of)
    return adapter_of


def got_adapters(head, both):
    slots, wide = head.shape
    slot = lax.broadcasted_iota(i32, (slots, wide), 0)
    named = jnp.sum(jnp.where(slot == slots - 1, head.astype(f32), 0.0), axis=0, keepdims=True)
    col = lax.broadcasted_iota(i32, (slots, wide), 1)
    across = jnp.sum(jnp.where(slot == col, named, 0.0), axis=1, keepdims=True)
    return jnp.broadcast_to(across, (slots, both)).astype(i32)


def which_adapters(adapt_dev, me_ref, len_ref, id_ref, head_refs, shape):
    if head_refs:
        return got_adapters(head_refs[0][...], shape[1])
    return own_adapters(list(requests(len_ref, id_ref, me_ref[0], adapt_dev)), *shape)


def low_kernel(adapt_dev, rank, plan, block, heads_in, x_count, first, final, me_ref, len_ref, id_ref, *refs):
    head_refs, refs = refs[:heads_in], refs[heads_in:]
    x_refs, refs, out_ref = refs[:x_count], refs[x_count:-1], refs[-1]
    which = which_adapters(adapt_dev, me_ref, len_ref, id_ref, head_refs, out_ref.shape)
    me = me_ref[0]
    total = jnp.zeros(out_ref.shape, f32) if first else refs[-1][...]
    for m, ref_no, blocks in plan:
        term = None
        for start, col, size in blocks:
            for j in range(0, size, block):
                down = refs[ref_no][:, col + j : col + j + block]
                more = dot(x_refs[(start + j) // block][...], down, (1, 1))
                term = more if term is None else term + more
        total = total + jnp.where(which // adapt_dev == (me ^ m), term, 0.0)
    if final:
        lane = lax.broadcasted_iota(i32, out_ref.shape, 1)
        total = jnp.where(which % adapt_dev == lane // rank, total, 0.0)
    out_ref[...] = total


def up_kernel(adapt_dev, marks, heads_in, me_ref, len_ref, id_ref, *refs):
    head_refs, refs = refs[:heads_in], refs[heads_in:]
    part_ref, other_ref, *refs, out_ref = refs
    which = which_adapters(adapt_dev, me_ref, len_ref, id_ref, head_refs, part_ref.shape)
    low = (part_ref[...] + other_ref[...]).astype(bf16).astype(f32)
    total = None
    for m, up_ref in zip(marks, refs):
        term = dot(jnp.where(which // adapt_dev == (me_ref[0] ^ m), low, 0.0).astype(bf16), up_ref[...])
        total = term if total is None else total + term
    delta = total.astype(bf16)
    if heads_in:
        out_ref[...] = delta
    else:
        out_ref[...] = refs[-1][...] + adapter_scale * delta.astype(f32)


def last_kernel(adapt_dev, me_ref, len_ref, id_ref, sum_ref, back_ref, out_ref):
    rows, slots = sum_ref.shape[0], back_ref.shape[0]
    reqs = list(requests(len_ref, id_ref, me_ref[0], adapt_dev))
    hit = row_places(reqs, (rows, slots), 0) == lax.broadcasted_iota(i32, (rows, slots), 1)
    delta = dot(hit.astype(f32).astype(bf16), back_ref[...])
    out_ref[...] = (sum_ref[...] + adapter_scale * delta).astype(bf16)


def whole(x):
    return pl.BlockSpec(x.shape, lambda *_: (0,) * x.ndim)


def columns(x, start, size):
    return pl.BlockSpec((x.shape[0], size), lambda *_: (0, start // size))


def after(x, *others):
    return lax.optimization_barrier((x, *others))[0]


def shards(tokens, kv_weight, down_a, up_weight, adapter_ids, lengths):
    owners = lax.axis_size("adapter")
    core = lax.axis_index("tensor")
    adapt_dev, width, rank = down_a.shape
    both = adapt_dev * rank
    rows, half = tokens.shape
    heads = kv_weight.shape[1]
    req_dev = lengths.shape[0]
    most = 2 * rows // req_dev
    cold = -(-(rows - most) // (req_dev - 1))
    slots = min(rows, most + (owners // 2 - 1) * cold) + 1
    slots = -(-slots // 8) * 8
    head_wide = -(-slots // 128) * 128
    me = lax.axis_index("adapter").astype(i32).reshape(1)
    scalars = (me, lengths, adapter_ids)
    params = pltpu.CompilerParams(vmem_limit_bytes=vmem_limit)

    def flip(x, bit):
        return lax.ppermute(x, "adapter", [(j, j ^ bit) for j in range(owners)])

    def other_core(x):
        return lax.ppermute(x, "tensor", [(0, 1), (1, 0)])

    sizes = [half * p // 16 for p in chunk_parts]
    spans = [(sum(sizes[:c]), size) for c, size in enumerate(sizes)]
    widths = [size + (heads if c == up_chunk else 0) for c, size in enumerate(sizes)] + [half + heads]
    sent_shapes = [jax.ShapeDtypeStruct((slots, half // halves), bf16)] * halves
    *outs, mine = pl.pallas_call(
        functools.partial(start_kernel, adapt_dev, spans, up_chunk),
        grid=(halves,),
        out_shape=sent_shapes + [jax.ShapeDtypeStruct((both, w), bf16) for w in widths],
        in_specs=[smem] * 2
        + [pl.BlockSpec((rows, half // halves), lambda g: (0, g))]
        + [pl.BlockSpec(memory_space=pl.ANY)] * 2,
        out_specs=[pl.BlockSpec((slots, half // halves), lambda *_: (0, 0))] * halves
        + [pl.BlockSpec((both, w), lambda *_: (0, 0)) for w in widths],
        scratch_shapes=[pltpu.SemaphoreType.DMA((len(spans) + 3,))],
        compiler_params=pltpu.CompilerParams(vmem_limit_bytes=60 * 1024 * 1024),
        name="start",
    )(lengths, adapter_ids, tokens, jnp.transpose(down_a, (0, 2, 1)).reshape(both, width), up_weight.reshape(both, -1))
    sent, parts = outs[:halves], outs[halves:]
    tokens_other = other_core(after(tokens, sent[0]))
    got = [flip(after(x, tokens_other), swap_bit) for x in sent]

    bits = [1 << b for b in range(owners.bit_length() - 1)]
    whole_places = [(c, heads + a) for c, (a, _) in enumerate(spans)]
    split = [(part, [(c, heads if c == up_chunk else 0)]) for c, part in enumerate(parts)]
    pieces = {0: [(mine, whole_places)]}
    for bit in [b for b in bits if b > swap_bit]:
        for m in list(pieces):
            came = []
            for c, (x, places) in enumerate(split if m == 0 else pieces[m]):
                came.append((flip(after(x, came[0][0]) if c == 2 else x, bit), places))
            pieces[m | bit] = came
    near = flip(mine, 1)

    base_own = dot(tokens, lax.dynamic_slice(kv_weight, (core * half, 0), (half, heads)))
    base = base_own + dot(tokens_other, lax.dynamic_slice(kv_weight, ((1 - core) * half, 0), (half, heads)))

    def add_low(arrays, heads_in, sums, group, final=False):
        used = sorted({c for _, _, places in group for c, _ in places})
        lowest, above = spans[used[0]][0], sum(spans[used[-1]])
        block = math.gcd(half // halves, *(edge for c in used for edge in spans[c]), lowest)
        at = range(lowest, above, block)
        plan = [
            (m, k, [(spans[c][0] - lowest, col, spans[c][1]) for c, col in places])
            for k, (m, _, places) in enumerate(group)
        ]
        xs = [arrays[a * len(arrays) // half] for a in at]
        x_specs = [columns(x, a % x.shape[1], block) for x, a in zip(xs, at, strict=True)]
        tail = [x for _, x, _ in group] + ([] if sums is None else [sums])
        n = arrays[0].shape[0]
        flops = sum(2 * n * both * size for _, _, blocks in plan for _, _, size in blocks)
        return pl.pallas_call(
            functools.partial(
                low_kernel, adapt_dev, rank, plan, block, len(heads_in), len(xs), sums is None, final
            ),
            grid=(1,),
            out_shape=jax.ShapeDtypeStruct((n, both), f32),
            in_specs=[smem] * 3 + [columns(x, 0, head_wide) for x in heads_in] + x_specs + [whole(x) for x in tail],
            out_specs=pl.BlockSpec((n, both), lambda *_: (0, 0)),
            compiler_params=params,
            cost_estimate=pl.CostEstimate(flops=4 * flops, bytes_accessed=flops // 64, transcendentals=0),
            name="low",
        )(*scalars, *heads_in, *xs, *tail)

    pieces[1] = [(near, whole_places)]
    far = [(m, x, places) for m, piece in pieces.items() if m & ~1 and not m & 1 for x, places in piece]
    far.sort(key=lambda item: item[2][0][0])
    items = [(0, mine, whole_places), (1, near, whole_places), far[0]]
    own = add_low([tokens], [], None, items)
    done = len(items)
    for k, (m, x, places) in enumerate(far):
        last = places[0][0] == len(spans) - 1
        if False:
            own, done = add_low([tokens], [], own, items[3:5]), 5
        across = flip(after(x, own, base) if last else after(x, own if k else base_own), 1)
        pieces.setdefault(m | 1, []).append((across, places))
        items.extend([(m, x, places), (m | 1, across, places)][0 if k else 1 :])

    def low_rank(arrays, heads_in, sums, todo, batch, final):
        rest = len(todo) - final
        for a in range(0, rest, batch):
            sums = add_low(arrays, heads_in, sums, todo[a : min(a + batch, rest)])
        part = add_low(arrays, heads_in, sums, todo[rest:], True)
        return part, other_core(part)

    ups = [next(x for x, places in piece if (up_chunk, heads) == places[-1] or len(places) > 1) for piece in pieces.values()]

    def up(heads_in, lows, extra, kind):
        n = lows[0].shape[0]
        return pl.pallas_call(
            functools.partial(up_kernel, adapt_dev, list(pieces), len(heads_in)),
            grid=(1,),
            out_shape=jax.ShapeDtypeStruct((n, heads), kind),
            in_specs=[smem] * 3
            + [columns(x, 0, head_wide) for x in heads_in]
            + [whole(x) for x in lows]
            + [columns(x, 0, heads) for x in ups]
            + [whole(x) for x in extra],
            out_specs=pl.BlockSpec((n, heads), lambda *_: (0, 0)),
            compiler_params=params,
            name="up",
        )(*scalars, *heads_in, *lows, *ups, *extra)

    low_got = low_rank(got, got[:1], None, items, max(6, owners // 8), 2)
    delta_got = up(got[:1], low_got, [], bf16)
    back = flip(delta_got, swap_bit)
    low_own = low_rank([tokens], [], after(own, delta_got), items[done:], max(5, owners // 8), 5)
    total = up([], low_own, [base], f32)
    return pl.pallas_call(
        functools.partial(last_kernel, adapt_dev),
        grid=(1,),
        out_shape=jax.ShapeDtypeStruct((rows, heads), bf16),
        in_specs=[smem] * 3 + [whole(total), whole(back)],
        out_specs=pl.BlockSpec((rows, heads), lambda *_: (0, 0)),
        compiler_params=params,
        name="last",
    )(*scalars, total, back)


def solution(mesh):
    placed = (
        P(("groups", "adapter"), "tensor"),
        P(None, "tensor"),
        P(("groups", "adapter"), None, None),
        P(("groups", "adapter"), None, None),
        P(("groups", "adapter")),
        P(("groups", "adapter")),
    )
    return jax.shard_map(
        shards,
        mesh=mesh,
        in_specs=placed,
        out_specs=P(("groups", "adapter"), "tensor"),
        check_vma=False,
    )
```

```python
import functools
import math

import jax
import jax.numpy as jnp
from jax import lax
from jax.experimental import pallas as pl
from jax.experimental.pallas import tpu as pltpu
from jax.sharding import PartitionSpec as P

adapter_scale = 2.0
bf16 = jnp.bfloat16
f32 = jnp.float32
i32 = jnp.int32
swap_bit = 2
chunk_parts = (6, 6, 4)
halves = 2
vmem_limit = 48 * 1024 * 1024
smem = pl.BlockSpec(memory_space=pltpu.SMEM)


def dot(left, right, contract=(1, 0)):
    return lax.dot_general(left, right, ((contract[:1], contract[1:]), ((), ())), preferred_element_type=f32)


def requests(len_ref, id_ref, me, adapt_dev):
    first, slot = 0, 0
    for q in range(len_ref.shape[0]):
        length, adapter = len_ref[q], id_ref[q]
        away = jnp.where((((adapter // adapt_dev) ^ me) & swap_bit) != 0, length, 0)
        yield first, length, adapter, slot, away
        first, slot = first + length, slot + away


def row_places(reqs, shape, dim):
    r = lax.broadcasted_iota(i32, shape, dim)
    place = jnp.full(shape, -1, i32)
    for first, _, _, slot, away in reqs:
        place = jnp.where((r >= first) & (r < first + away), r - first + slot, place)
    return place


def cut_kernel(cuts, down_ref, up_ref, *refs):
    *out_refs, stage_ref, sems = refs
    cores = lax.axis_size("tensor")
    heads, half = up_ref.shape[1] // cores, down_ref.shape[1] // cores
    core = lax.axis_index("tensor")
    features = down_ref.at[:, pl.ds(pl.multiple_of(core * half, 128), half)]
    up = up_ref.at[:, pl.ds(pl.multiple_of(core * heads, 128), heads)]
    moves = [(features, stage_ref.at[:, pl.ds(heads, half)]), (up, stage_ref.at[:, pl.ds(0, heads)])]
    for (start, size), out_ref in zip(cuts, out_refs):
        moves.append((stage_ref.at[:, pl.ds(start, size)], out_ref))
    copies = [pltpu.make_async_copy(source, target, sems.at[k]) for k, (source, target) in enumerate(moves)]
    for copy in copies[:2]:
        copy.start()
    for copy in copies[:2]:
        copy.wait()
    for copy in copies[2:]:
        copy.start()
    for copy in copies[2:]:
        copy.wait()


def pack_kernel(adapt_dev, me_ref, len_ref, id_ref, tok_ref, *sent_refs):
    slots, step = sent_refs[0].shape
    rows = tok_ref.shape[0]
    reqs = list(requests(len_ref, id_ref, me_ref[0], adapt_dev))
    hit = lax.broadcasted_iota(i32, (slots, rows), 0) == row_places(reqs, (1, rows), 1)
    pick = hit.astype(f32).astype(bf16)
    last = lax.broadcasted_iota(i32, (slots, step), 0) == slots - 1
    for part, sent_ref in enumerate(sent_refs):
        packed = dot(pick, tok_ref[:, part * step : (part + 1) * step])
        if part * step < slots:
            col = lax.broadcasted_iota(i32, (1, step), 1) + part * step
            adapter_of = jnp.zeros((1, step), i32)
            for _, _, adapter, slot, away in reqs:
                adapter_of = jnp.where((col >= slot) & (col < slot + away), adapter, adapter_of)
            packed = jnp.where(last, adapter_of.astype(f32), packed)
        sent_ref[...] = packed.astype(bf16)


def own_adapters(reqs, rows, both):
    r = lax.broadcasted_iota(i32, (rows, both), 0)
    adapter_of = jnp.zeros((rows, both), i32)
    for first, length, adapter, _, _ in reqs:
        adapter_of = jnp.where((r >= first) & (r < first + length), adapter, adapter_of)
    return adapter_of


def got_adapters(head, both):
    slots, wide = head.shape
    slot = lax.broadcasted_iota(i32, (slots, wide), 0)
    named = jnp.sum(jnp.where(slot == slots - 1, head.astype(f32), 0.0), axis=0, keepdims=True)
    col = lax.broadcasted_iota(i32, (slots, wide), 1)
    across = jnp.sum(jnp.where(slot == col, named, 0.0), axis=1, keepdims=True)
    return jnp.broadcast_to(across, (slots, both)).astype(i32)


def which_adapters(adapt_dev, me_ref, len_ref, id_ref, head_refs, shape):
    if head_refs:
        return got_adapters(head_refs[0][...], shape[1])
    return own_adapters(list(requests(len_ref, id_ref, me_ref[0], adapt_dev)), *shape)


def low_kernel(adapt_dev, rank, plan, heads_in, x_count, first, final, me_ref, len_ref, id_ref, *refs):
    head_refs, refs = refs[:heads_in], refs[heads_in:]
    x_refs, refs, out_ref = refs[:x_count], refs[x_count:-1], refs[-1]
    which = which_adapters(adapt_dev, me_ref, len_ref, id_ref, head_refs, out_ref.shape)
    me = me_ref[0]
    total = jnp.zeros(out_ref.shape, f32) if first else refs[-1][...]
    for m, pairs in plan:
        term = None
        for x_no, ref_no in pairs:
            more = dot(x_refs[x_no][...], refs[ref_no][...], (1, 1))
            term = more if term is None else term + more
        total = total + jnp.where(which // adapt_dev == (me ^ m), term, 0.0)
    if final:
        lane = lax.broadcasted_iota(i32, out_ref.shape, 1)
        total = jnp.where(which % adapt_dev == lane // rank, total, 0.0)
    out_ref[...] = total


def up_kernel(adapt_dev, marks, heads_in, me_ref, len_ref, id_ref, *refs):
    head_refs, refs = refs[:heads_in], refs[heads_in:]
    part_ref, other_ref, *refs, out_ref = refs
    which = which_adapters(adapt_dev, me_ref, len_ref, id_ref, head_refs, part_ref.shape)
    low = (part_ref[...] + other_ref[...]).astype(bf16).astype(f32)
    total = None
    for m, up_ref in zip(marks, refs):
        term = dot(jnp.where(which // adapt_dev == (me_ref[0] ^ m), low, 0.0).astype(bf16), up_ref[...])
        total = term if total is None else total + term
    delta = total.astype(bf16)
    if heads_in:
        out_ref[...] = delta
    else:
        out_ref[...] = refs[-1][...] + adapter_scale * delta.astype(f32)


def last_kernel(adapt_dev, me_ref, len_ref, id_ref, sum_ref, back_ref, out_ref):
    rows, slots = sum_ref.shape[0], back_ref.shape[0]
    reqs = list(requests(len_ref, id_ref, me_ref[0], adapt_dev))
    hit = row_places(reqs, (rows, slots), 0) == lax.broadcasted_iota(i32, (rows, slots), 1)
    delta = dot(hit.astype(f32).astype(bf16), back_ref[...])
    out_ref[...] = (sum_ref[...] + adapter_scale * delta).astype(bf16)


def whole(x):
    return pl.BlockSpec(x.shape, lambda *_: (0,) * x.ndim)


def columns(x, start, size):
    return pl.BlockSpec((x.shape[0], size), lambda *_: (0, start // size))


def after(x, *others):
    return lax.optimization_barrier((x, *others))[0]


def shards(tokens, kv_weight, down_a, up_weight, adapter_ids, lengths):
    owners = lax.axis_size("adapter")
    core = lax.axis_index("tensor")
    adapt_dev, width, rank = down_a.shape
    both = adapt_dev * rank
    rows, half = tokens.shape
    heads = kv_weight.shape[1]
    req_dev = lengths.shape[0]
    most = 2 * rows // req_dev
    cold = -(-(rows - most) // (req_dev - 1))
    slots = min(rows, most + (owners // 2 - 1) * cold) + 1
    slots = -(-slots // 8) * 8
    head_wide = -(-slots // 128) * 128
    me = lax.axis_index("adapter").astype(i32).reshape(1)
    scalars = (me, lengths, adapter_ids)
    params = pltpu.CompilerParams(vmem_limit_bytes=vmem_limit)

    def flip(x, bit):
        return lax.ppermute(x, "adapter", [(j, j ^ bit) for j in range(owners)])

    def other_core(x):
        return lax.ppermute(x, "tensor", [(0, 1), (1, 0)])

    sizes = [half * p // 16 for p in chunk_parts]
    spans = [(sum(sizes[:c]), size) for c, size in enumerate(sizes)]
    cuts = [(a + (heads if c else 0), size + (0 if c else heads)) for c, (a, size) in enumerate(spans)]
    cuts.append((0, heads + half))
    *parts, mine = pl.pallas_call(
        functools.partial(cut_kernel, cuts),
        out_shape=[jax.ShapeDtypeStruct((both, w), bf16) for _, w in cuts],
        in_specs=[pl.BlockSpec(memory_space=pl.ANY)] * 2,
        out_specs=[pl.BlockSpec(memory_space=pl.ANY)] * len(cuts),
        scratch_shapes=[pltpu.VMEM((both, heads + half), bf16), pltpu.SemaphoreType.DMA((2 + len(cuts),))],
        compiler_params=pltpu.CompilerParams(vmem_limit_bytes=60 * 1024 * 1024),
        name="cut",
    )(jnp.transpose(down_a, (0, 2, 1)).reshape(both, width), up_weight.reshape(both, -1))
    tokens_other = other_core(after(tokens, mine))
    sent = pl.pallas_call(
        functools.partial(pack_kernel, adapt_dev),
        grid=(1,),
        out_shape=[jax.ShapeDtypeStruct((slots, half // halves), bf16)] * halves,
        in_specs=[smem] * 3 + [whole(tokens)],
        out_specs=[pl.BlockSpec((slots, half // halves), lambda *_: (0, 0))] * halves,
        compiler_params=pltpu.CompilerParams(vmem_limit_bytes=60 * 1024 * 1024),
        name="pack",
    )(*scalars, after(tokens, mine))
    got = [flip(after(x, tokens_other), swap_bit) for x in sent]

    bits = [1 << b for b in range(owners.bit_length() - 1)]
    whole_places = [(c, heads + a) for c, (a, _) in enumerate(spans)]
    split = [(part, [(c, 0 if c else heads)]) for c, part in enumerate(parts)]
    pieces = {0: [(mine, whole_places)]}
    for bit in [b for b in bits if b > swap_bit]:
        for m in list(pieces):
            came = []
            for c, (x, places) in enumerate(split if m == 0 else pieces[m]):
                came.append((flip(after(x, came[0][0]) if c == 2 else x, bit), places))
            pieces[m | bit] = came
    near = flip(mine, 1)

    base_own = dot(after(tokens, *sent), lax.dynamic_slice(kv_weight, (core * half, 0), (half, heads)))
    base = base_own + dot(tokens_other, lax.dynamic_slice(kv_weight, ((1 - core) * half, 0), (half, heads)))

    def add_low(arrays, heads_in, sums, group, final=False, within=(0, half)):
        takes = []
        for m, x, places in group:
            for c, col in places:
                start, size = spans[c]
                low, high = max(start, within[0]), min(start + size, within[1])
                if low < high:
                    takes.append((m, x, low, high, col - start))
        block = math.gcd(half // halves, *(n for _, _, low, high, shift in takes for n in (low, high, shift)))
        at = sorted({a for _, _, low, high, _ in takes for a in range(low, high, block)})
        plan, tail, specs = [], [], []
        for m, x, low, high, shift in takes:
            pairs = []
            for a in range(low, high, block):
                pairs.append((at.index(a), len(tail)))
                tail.append(x)
                specs.append(columns(x, a + shift, block))
            plan.append((m, pairs))
        xs = [arrays[a * len(arrays) // half] for a in at]
        x_specs = [columns(x, a % x.shape[1], block) for x, a in zip(xs, at, strict=True)]
        if sums is not None:
            tail, specs = tail + [sums], specs + [whole(sums)]
        n = arrays[0].shape[0]
        flops = sum(2 * n * both * block * len(pairs) for _, pairs in plan)
        return pl.pallas_call(
            functools.partial(low_kernel, adapt_dev, rank, plan, len(heads_in), len(xs), sums is None, final),
            grid=(1,),
            out_shape=jax.ShapeDtypeStruct((n, both), f32),
            in_specs=[smem] * 3 + [columns(x, 0, head_wide) for x in heads_in] + x_specs + specs,
            out_specs=pl.BlockSpec((n, both), lambda *_: (0, 0)),
            compiler_params=params,
            cost_estimate=pl.CostEstimate(flops=4 * flops, bytes_accessed=flops // 64, transcendentals=0),
            name="low",
        )(*scalars, *heads_in, *xs, *tail)

    pieces[1] = [(near, whole_places)]
    far = [(m, x, places) for m, piece in pieces.items() if m & ~1 and not m & 1 for x, places in piece]
    far.sort(key=lambda item: item[2][0][0])
    items = [(0, mine, whole_places), (1, near, whole_places), far[0]]
    own = add_low([tokens], [], None, items)
    done = len(items)
    for k, (m, x, places) in enumerate(far):
        last = places[0][0] == len(spans) - 1
        across = flip(after(x, own, base) if last else after(x, own if k else base_own), 1)
        pieces.setdefault(m | 1, []).append((across, places))
        items.extend([(m, x, places), (m | 1, across, places)][0 if k else 1 :])

    def low_rank(arrays, heads_in, sums, todo, batch, final):
        rest = len(todo) - final
        cut = half // len(arrays)
        for k in range(len(arrays)):
            for a in range(0, rest, batch):
                group = todo[a : min(a + batch, rest)]
                sums = add_low(arrays, heads_in, sums, group, within=(k * cut, (k + 1) * cut))
        part = add_low(arrays, heads_in, sums, todo[rest:], True)
        return part, other_core(part)

    ups = [piece[0][0] for piece in pieces.values()]

    def up(heads_in, lows, extra, kind):
        n = lows[0].shape[0]
        return pl.pallas_call(
            functools.partial(up_kernel, adapt_dev, list(pieces), len(heads_in)),
            grid=(1,),
            out_shape=jax.ShapeDtypeStruct((n, heads), kind),
            in_specs=[smem] * 3
            + [columns(x, 0, head_wide) for x in heads_in]
            + [whole(x) for x in lows]
            + [columns(x, 0, heads) for x in ups]
            + [whole(x) for x in extra],
            out_specs=pl.BlockSpec((n, heads), lambda *_: (0, 0)),
            compiler_params=params,
            name="up",
        )(*scalars, *heads_in, *lows, *ups, *extra)

    low_got = low_rank(got, got[:1], None, items, max(6, owners // 8), 2)
    delta_got = up(got[:1], low_got, [], bf16)
    back = flip(delta_got, swap_bit)
    low_own = low_rank([tokens], [], after(own, delta_got), items[done:], max(5, owners // 8), 5)
    total = up([], low_own, [base], f32)
    return pl.pallas_call(
        functools.partial(last_kernel, adapt_dev),
        grid=(1,),
        out_shape=jax.ShapeDtypeStruct((rows, heads), bf16),
        in_specs=[smem] * 3 + [whole(total), whole(back)],
        out_specs=pl.BlockSpec((rows, heads), lambda *_: (0, 0)),
        compiler_params=params,
        name="last",
    )(*scalars, total, back)


def solution(mesh):
    placed = (
        P(("groups", "adapter"), "tensor"),
        P(None, "tensor"),
        P(("groups", "adapter"), None, None),
        P(("groups", "adapter"), None, None),
        P(("groups", "adapter")),
        P(("groups", "adapter")),
    )
    return jax.shard_map(
        shards,
        mesh=mesh,
        in_specs=placed,
        out_specs=P(("groups", "adapter"), "tensor"),
        check_vma=False,
    )
```

```python
import functools
import math

import jax
import jax.numpy as jnp
from jax import lax
from jax.experimental import pallas as pl
from jax.experimental.pallas import tpu as pltpu
from jax.sharding import PartitionSpec as P

adapter_scale = 2.0
bf16 = jnp.bfloat16
f32 = jnp.float32
i32 = jnp.int32
swap_bit = 2
chunk_parts = (6, 6, 4)
halves = 2
vmem_limit = 24 * 1024 * 1024
smem = pl.BlockSpec(memory_space=pltpu.SMEM)


def dot(left, right, contract=(1, 0)):
    return lax.dot_general(left, right, ((contract[:1], contract[1:]), ((), ())), preferred_element_type=f32)


def requests(len_ref, id_ref, me, adapt_dev):
    first, slot = 0, 0
    for q in range(len_ref.shape[0]):
        length, adapter = len_ref[q], id_ref[q]
        away = jnp.where((((adapter // adapt_dev) ^ me) & swap_bit) != 0, length, 0)
        yield first, length, adapter, slot, away
        first, slot = first + length, slot + away


def row_places(reqs, shape, dim):
    r = lax.broadcasted_iota(i32, shape, dim)
    place = jnp.full(shape, -1, i32)
    for first, _, _, slot, away in reqs:
        place = jnp.where((r >= first) & (r < first + away), r - first + slot, place)
    return place


def cut_kernel(cuts, down_ref, up_ref, *refs):
    *out_refs, stage_ref, sems = refs
    cores = lax.axis_size("tensor")
    heads, half = up_ref.shape[1] // cores, down_ref.shape[1] // cores
    core = lax.axis_index("tensor")
    up = up_ref.at[:, pl.ds(pl.multiple_of(core * heads, 128), heads)]
    ins = [(up, stage_ref.at[:, pl.ds(0, heads)])]
    for c, (start, size) in enumerate(cuts[:-1]):
        ahead = 0 if c else heads
        at, size = start + ahead, size - ahead
        source = down_ref.at[:, pl.ds(pl.multiple_of(core * half + at - heads, 128), size)]
        ins.append((source, stage_ref.at[:, pl.ds(at, size)]))
    outs = [(stage_ref.at[:, pl.ds(start, size)], out_ref) for (start, size), out_ref in zip(cuts, out_refs)]
    copies = [pltpu.make_async_copy(source, target, sems.at[k]) for k, (source, target) in enumerate(ins + outs)]
    for copy in copies[: len(ins)]:
        copy.start()
    copies[0].wait()
    for arrived, leaving in zip(copies[1 : len(ins)], copies[len(ins) :]):
        arrived.wait()
        leaving.start()
    copies[-1].start()
    for copy in copies[len(ins) :]:
        copy.wait()


def pack_kernel(adapt_dev, me_ref, len_ref, id_ref, tok_ref, *sent_refs):
    slots, step = sent_refs[0].shape
    rows = tok_ref.shape[0]
    reqs = list(requests(len_ref, id_ref, me_ref[0], adapt_dev))
    hit = lax.broadcasted_iota(i32, (slots, rows), 0) == row_places(reqs, (1, rows), 1)
    pick = hit.astype(f32).astype(bf16)
    last = lax.broadcasted_iota(i32, (slots, step), 0) == slots - 1
    for part, sent_ref in enumerate(sent_refs):
        packed = dot(pick, tok_ref[:, part * step : (part + 1) * step])
        if part * step < slots:
            col = lax.broadcasted_iota(i32, (1, step), 1) + part * step
            adapter_of = jnp.zeros((1, step), i32)
            for _, _, adapter, slot, away in reqs:
                adapter_of = jnp.where((col >= slot) & (col < slot + away), adapter, adapter_of)
            packed = jnp.where(last, adapter_of.astype(f32), packed)
        sent_ref[...] = packed.astype(bf16)


def own_adapters(reqs, rows, both):
    r = lax.broadcasted_iota(i32, (rows, both), 0)
    adapter_of = jnp.zeros((rows, both), i32)
    for first, length, adapter, _, _ in reqs:
        adapter_of = jnp.where((r >= first) & (r < first + length), adapter, adapter_of)
    return adapter_of


def got_adapters(head, both):
    slots, wide = head.shape
    slot = lax.broadcasted_iota(i32, (slots, wide), 0)
    named = jnp.sum(jnp.where(slot == slots - 1, head.astype(f32), 0.0), axis=0, keepdims=True)
    col = lax.broadcasted_iota(i32, (slots, wide), 1)
    across = jnp.sum(jnp.where(slot == col, named, 0.0), axis=1, keepdims=True)
    return jnp.broadcast_to(across, (slots, both)).astype(i32)


def which_adapters(adapt_dev, me_ref, len_ref, id_ref, head_refs, shape):
    if head_refs:
        return got_adapters(head_refs[0][...], shape[1])
    return own_adapters(list(requests(len_ref, id_ref, me_ref[0], adapt_dev)), *shape)


def low_kernel(adapt_dev, rank, plan, heads_in, x_count, first, final, me_ref, len_ref, id_ref, *refs):
    head_refs, refs = refs[:heads_in], refs[heads_in:]
    x_refs, refs, out_ref = refs[:x_count], refs[x_count:-1], refs[-1]
    which = which_adapters(adapt_dev, me_ref, len_ref, id_ref, head_refs, out_ref.shape)
    me = me_ref[0]
    total = jnp.zeros(out_ref.shape, f32) if first else refs[-1][...]
    for m, pairs in plan:
        term = None
        for x_no, ref_no in pairs:
            more = dot(x_refs[x_no][...], refs[ref_no][...], (1, 1))
            term = more if term is None else term + more
        total = total + jnp.where(which // adapt_dev == (me ^ m), term, 0.0)
    if final:
        lane = lax.broadcasted_iota(i32, out_ref.shape, 1)
        total = jnp.where(which % adapt_dev == lane // rank, total, 0.0)
    out_ref[...] = total


def up_kernel(adapt_dev, marks, heads_in, me_ref, len_ref, id_ref, *refs):
    head_refs, refs = refs[:heads_in], refs[heads_in:]
    part_ref, other_ref, *refs, out_ref = refs
    which = which_adapters(adapt_dev, me_ref, len_ref, id_ref, head_refs, part_ref.shape)
    low = (part_ref[...] + other_ref[...]).astype(bf16).astype(f32)
    total = None
    for m, up_ref in zip(marks, refs):
        term = dot(jnp.where(which // adapt_dev == (me_ref[0] ^ m), low, 0.0).astype(bf16), up_ref[...])
        total = term if total is None else total + term
    delta = total.astype(bf16)
    if heads_in:
        out_ref[...] = delta
    else:
        out_ref[...] = refs[-1][...] + adapter_scale * delta.astype(f32)


def last_kernel(adapt_dev, me_ref, len_ref, id_ref, sum_ref, back_ref, out_ref):
    rows, slots = sum_ref.shape[0], back_ref.shape[0]
    reqs = list(requests(len_ref, id_ref, me_ref[0], adapt_dev))
    hit = row_places(reqs, (rows, slots), 0) == lax.broadcasted_iota(i32, (rows, slots), 1)
    delta = dot(hit.astype(f32).astype(bf16), back_ref[...])
    out_ref[...] = (sum_ref[...] + adapter_scale * delta).astype(bf16)


def whole(x):
    return pl.BlockSpec(x.shape, lambda *_: (0,) * x.ndim)


def columns(x, start, size):
    return pl.BlockSpec((x.shape[0], size), lambda *_: (0, start // size))


def after(x, *others):
    return lax.optimization_barrier((x, *others))[0]


def shards(tokens, kv_weight, down_a, up_weight, adapter_ids, lengths):
    owners = lax.axis_size("adapter")
    core = lax.axis_index("tensor")
    adapt_dev, width, rank = down_a.shape
    both = adapt_dev * rank
    rows, half = tokens.shape
    heads = kv_weight.shape[1]
    req_dev = lengths.shape[0]
    most = 2 * rows // req_dev
    cold = -(-(rows - most) // (req_dev - 1))
    slots = min(rows, most + (owners // 2 - 1) * cold) + 1
    slots = -(-slots // 8) * 8
    head_wide = -(-slots // 128) * 128
    me = lax.axis_index("adapter").astype(i32).reshape(1)
    scalars = (me, lengths, adapter_ids)
    params = pltpu.CompilerParams(vmem_limit_bytes=vmem_limit)

    def flip(x, bit):
        return lax.ppermute(x, "adapter", [(j, j ^ bit) for j in range(owners)])

    def other_core(x):
        return lax.ppermute(x, "tensor", [(0, 1), (1, 0)])

    sizes = [half * p // 16 for p in chunk_parts]
    spans = [(sum(sizes[:c]), size) for c, size in enumerate(sizes)]
    cuts = [(a + (heads if c else 0), size + (0 if c else heads)) for c, (a, size) in enumerate(spans)]
    cuts.append((0, heads + half))
    *parts, mine = pl.pallas_call(
        functools.partial(cut_kernel, cuts),
        out_shape=[jax.ShapeDtypeStruct((both, w), bf16) for _, w in cuts],
        in_specs=[pl.BlockSpec(memory_space=pl.ANY)] * 2,
        out_specs=[pl.BlockSpec(memory_space=pl.ANY)] * len(cuts),
        scratch_shapes=[pltpu.VMEM((both, heads + half), bf16), pltpu.SemaphoreType.DMA((2 * len(cuts),))],
        compiler_params=pltpu.CompilerParams(vmem_limit_bytes=60 * 1024 * 1024),
        name="cut",
    )(jnp.transpose(down_a, (0, 2, 1)).reshape(both, width), up_weight.reshape(both, -1))
    tokens_other = other_core(after(tokens, mine))
    sent = pl.pallas_call(
        functools.partial(pack_kernel, adapt_dev),
        grid=(1,),
        out_shape=[jax.ShapeDtypeStruct((slots, half // halves), bf16)] * halves,
        in_specs=[smem] * 3 + [whole(tokens)],
        out_specs=[pl.BlockSpec((slots, half // halves), lambda *_: (0, 0))] * halves,
        compiler_params=pltpu.CompilerParams(vmem_limit_bytes=60 * 1024 * 1024),
        name="pack",
    )(*scalars, after(tokens, mine))
    got = [flip(after(x, tokens_other), swap_bit) for x in sent]

    bits = [1 << b for b in range(owners.bit_length() - 1)]
    whole_places = [(c, heads + a) for c, (a, _) in enumerate(spans)]
    split = [(part, [(c, 0 if c else heads)]) for c, part in enumerate(parts)]
    pieces = {0: [(mine, whole_places)]}
    for bit in [b for b in bits if b > swap_bit]:
        for m in list(pieces):
            came = []
            for c, (x, places) in enumerate(split if m == 0 else pieces[m]):
                came.append((flip(after(x, came[0][0]) if c == 2 else x, bit), places))
            pieces[m | bit] = came
    near = flip(mine, 1)

    base_own = dot(after(tokens, *sent), lax.dynamic_slice(kv_weight, (core * half, 0), (half, heads)))
    base = base_own + dot(tokens_other, lax.dynamic_slice(kv_weight, ((1 - core) * half, 0), (half, heads)))

    def add_low(arrays, heads_in, sums, group, final=False, within=(0, half)):
        takes = []
        for m, x, places in group:
            for c, col in places:
                start, size = spans[c]
                low, high = max(start, within[0]), min(start + size, within[1])
                if low < high:
                    takes.append((m, x, low, high, col - start))
        block = math.gcd(half // halves, *(n for _, _, low, high, shift in takes for n in (low, high, shift)))
        at = sorted({a for _, _, low, high, _ in takes for a in range(low, high, block)})
        plan, tail, specs = [], [], []
        for m, x, low, high, shift in takes:
            pairs = []
            for a in range(low, high, block):
                pairs.append((at.index(a), len(tail)))
                tail.append(x)
                specs.append(columns(x, a + shift, block))
            plan.append((m, pairs))
        xs = [arrays[a * len(arrays) // half] for a in at]
        x_specs = [columns(x, a % x.shape[1], block) for x, a in zip(xs, at, strict=True)]
        if sums is not None:
            tail, specs = tail + [sums], specs + [whole(sums)]
        n = arrays[0].shape[0]
        flops = sum(2 * n * both * block * len(pairs) for _, pairs in plan)
        return pl.pallas_call(
            functools.partial(low_kernel, adapt_dev, rank, plan, len(heads_in), len(xs), sums is None, final),
            grid=(1,),
            out_shape=jax.ShapeDtypeStruct((n, both), f32),
            in_specs=[smem] * 3 + [columns(x, 0, head_wide) for x in heads_in] + x_specs + specs,
            out_specs=pl.BlockSpec((n, both), lambda *_: (0, 0)),
            compiler_params=params,
            cost_estimate=pl.CostEstimate(flops=4 * flops, bytes_accessed=flops // 64, transcendentals=0),
            name="low",
        )(*scalars, *heads_in, *xs, *tail)

    pieces[1] = [(near, whole_places)]
    far = [(m, x, places) for m, piece in pieces.items() if m & ~1 and not m & 1 for x, places in piece]
    far.sort(key=lambda item: item[2][0][0])
    items = [(0, mine, whole_places), (1, near, whole_places), far[0]]
    own = add_low([tokens], [], None, items)
    done = len(items)
    for k, (m, x, places) in enumerate(far):
        last = places[0][0] == len(spans) - 1
        across = flip(after(x, own, base) if last else after(x, own if k else base_own), 1)
        pieces.setdefault(m | 1, []).append((across, places))
        items.extend([(m, x, places), (m | 1, across, places)][0 if k else 1 :])

    def low_rank(arrays, heads_in, sums, todo, batch, final):
        rest = len(todo) - final
        cut = half // len(arrays)
        for k in range(len(arrays)):
            for a in range(0, rest, batch):
                group = todo[a : min(a + batch, rest)]
                sums = add_low(arrays, heads_in, sums, group, within=(k * cut, (k + 1) * cut))
        part = add_low(arrays, heads_in, sums, todo[rest:], True)
        return part, other_core(part)

    ups = [piece[0][0] for piece in pieces.values()]

    def up(heads_in, lows, extra, kind):
        n = lows[0].shape[0]
        return pl.pallas_call(
            functools.partial(up_kernel, adapt_dev, list(pieces), len(heads_in)),
            grid=(1,),
            out_shape=jax.ShapeDtypeStruct((n, heads), kind),
            in_specs=[smem] * 3
            + [columns(x, 0, head_wide) for x in heads_in]
            + [whole(x) for x in lows]
            + [columns(x, 0, heads) for x in ups]
            + [whole(x) for x in extra],
            out_specs=pl.BlockSpec((n, heads), lambda *_: (0, 0)),
            compiler_params=params,
            name="up",
        )(*scalars, *heads_in, *lows, *ups, *extra)

    low_got = low_rank(got, got[:1], None, items, max(6, owners // 8), 2)
    delta_got = up(got[:1], low_got, [], bf16)
    back = flip(delta_got, swap_bit)
    low_own = low_rank([tokens], [], after(own, delta_got), items[done:], max(5, owners // 8), 5)
    total = up([], low_own, [base], f32)
    return pl.pallas_call(
        functools.partial(last_kernel, adapt_dev),
        grid=(1,),
        out_shape=jax.ShapeDtypeStruct((rows, heads), bf16),
        in_specs=[smem] * 3 + [whole(total), whole(back)],
        out_specs=pl.BlockSpec((rows, heads), lambda *_: (0, 0)),
        compiler_params=params,
        name="last",
    )(*scalars, total, back)


def solution(mesh):
    placed = (
        P(("groups", "adapter"), "tensor"),
        P(None, "tensor"),
        P(("groups", "adapter"), None, None),
        P(("groups", "adapter"), None, None),
        P(("groups", "adapter")),
        P(("groups", "adapter")),
    )
    return jax.shard_map(
        shards,
        mesh=mesh,
        in_specs=placed,
        out_specs=P(("groups", "adapter"), "tensor"),
        check_vma=False,
    )
```
